32 devices in a mesh: row: 8 (over z, core), col: 4 (over y, x).
Axes of the slice: x: 2, y: 2, z: 4, core: 2. Of those that a mesh axis runs over, the one named last changes fastest.
Arguments:
- context: bfloat16 [128, 8192], P('col', 'row'), may hold values from -6 to 6
- weight: bfloat16 [8192, 16384], P('row', 'col'), may hold values from -0.0625 to 0.0625
- feature_bias: float32 [16384], P('col'), may hold values from -3 to 3
- covariance: float32 [16384, 16384], P('row', 'col'), may hold values from -0.5 to 2.5, as said below
- prior_mean: float32 [16384], P('row'), may hold values from -6 to 6
- rewards: float32 [128], replicated, may hold values from -12 to 12
Outputs:
- posterior_cov: float32 [16384, 16384], P('row', 'col')
- posterior_mean: float32 [16384], P('row')
The draws below stay inside these ranges and needn't reach their ends.
Inputs may be any that keep to these rules, and one draw needn't show every extreme that they name: covariance is exactly symmetric and positive definite.
All inputs are finite; a program needn't handle non-finite values.
Results may differ from the reference program's by a relative error of at most 0.00042.
Values may be sent and summed in bfloat16 or wider, within the bound.
No kernel may reach another device: no remote copies, remote signals or barrier semaphores. Data moves between devices by JAX's collectives and lax.ppermute only.
A program may use at most 128 MiB of HBM per device.

```python
import jax
import jax.numpy as jnp
from jax import lax

F = 16384
DM = 8192
B = 128


def draw_covariance(key, part):
    base = jax.random.fold_in(key, 7)
    first, second = jax.random.split(base)
    noise = jax.random.normal(first, (F, F), jnp.float32)
    symmetric = (noise + noise.T) * (0.25 / F ** 0.5)
    diagonal = jnp.exp(jax.random.uniform(second, (F,), jnp.float32, 0.0, 0.6931))
    return symmetric + jnp.diag(diagonal)


def block_scale(rng, shape, cuts, smallest, top_value):
    def one(position, parts):
        steps = jax.random.uniform(jax.random.fold_in(jax.random.fold_in(rng, 6), position), (parts,), jnp.float32, smallest / len(cuts), top_value / len(cuts))
        return jnp.repeat(jnp.exp(steps), shape[position] // parts).reshape((-1,) + (1,) * (len(shape) - position - 1))

    factor_of = one(*cuts[0])
    for cut in cuts[1:]:
        factor_of = factor_of * one(*cut)
    return factor_of


def centred(own_key, shape, spread, most, cuts=(), held_as=jnp.bfloat16):
    factor_of = block_scale(own_key, shape, cuts, -0.22, 0.18) if cuts else 1.0
    array = jax.random.normal(own_key, shape, jnp.float32) * spread * factor_of
    return jnp.minimum(jnp.maximum(array, -most), most).astype(held_as)


def setup_inputs(seed: int = 0) -> dict:
    streams_of = jax.random.split(jax.random.key(seed), 7)
    context = centred(streams_of[0], (B, DM), 1.0, 6.0, ((0, 4), (1, 8)))
    weight = centred(streams_of[1], (DM, F), DM ** -0.5, 0.0625, ((0, 8), (1, 4)))
    feature_bias = centred(streams_of[2], (F,), 0.5, 3.0, ((0, 4),), jnp.float32)
    covariance = draw_covariance(jax.random.fold_in(streams_of[6], 71), 0)
    prior_mean = centred(streams_of[4], (F,), 1.0, 6.0, ((0, 8),), jnp.float32)
    rewards = centred(streams_of[5], (B,), 2.0, 12.0, (), jnp.float32)
    return dict(context=context, weight=weight, feature_bias=feature_bias, covariance=covariance, prior_mean=prior_mean, rewards=rewards)


def reference(context, weight, feature_bias, covariance, prior_mean, rewards):
    highest = lax.Precision.HIGHEST
    preact = jnp.dot(context.astype(jnp.float32), weight.astype(jnp.float32), preferred_element_type=jnp.float32)
    features = jnp.tanh(preact + feature_bias[None, :]).astype(jnp.bfloat16)
    feat32 = features.astype(jnp.float32)
    panel = jnp.einsum('ik,bk->ib', covariance, feat32, precision=highest)
    gram_matrix = jnp.dot(feat32, panel, precision=highest) + jnp.eye(B, dtype=jnp.float32)
    predicted = jnp.dot(feat32, prior_mean, precision=highest)
    lower_factor = jnp.linalg.cholesky(gram_matrix)
    lower_inverse = lax.linalg.triangular_solve(lower_factor, jnp.eye(B, dtype=jnp.float32), left_side=True, lower=True)
    inverse_gram = jnp.dot(lower_inverse.T, lower_inverse, precision=highest)
    coeffs = jnp.dot(inverse_gram, rewards - predicted, precision=highest)
    gain = jnp.dot(panel, inverse_gram, precision=highest)
    posterior_mean = prior_mean + jnp.dot(panel, coeffs, precision=highest)
    posterior_cov = covariance - jnp.einsum('ib,jb->ij', gain, panel, precision=highest)
    return (posterior_cov, posterior_mean)
```

```python
import functools

import jax
import jax.numpy as jnp
from jax import lax
from jax.experimental import pallas as pl
from jax.experimental.pallas import tpu as pltpu
from jax.sharding import PartitionSpec as P

F32 = jnp.float32
BF16 = jnp.bfloat16
MIB = 1 << 20
NT = (((1,), (1,)), ((), ()))
TN = (((0,), (0,)), ((), ()))


def dot(a, b, dims=(((1,), (0,)), ((), ()))):
    return lax.dot_general(a, b, dims, preferred_element_type=F32)


def split2(x):
    hi = x.astype(BF16)
    return hi, (x - hi.astype(F32)).astype(BF16)


def split3(x):
    hi = x.astype(BF16)
    rest = x - hi.astype(F32)
    mid = rest.astype(BF16)
    return hi, mid, (rest - mid.astype(F32)).astype(BF16)


def vmem(n):
    return [pl.BlockSpec(memory_space=pltpu.VMEM)] * n


def broadcast(array, axis, root):
    mine = lax.axis_index(axis) == root
    return lax.psum(jnp.where(mine, array, jnp.zeros_like(array)), axis)


def plain(context, weight, feature_bias, covariance, prior_mean, rewards):
    highest = lax.Precision.HIGHEST
    group_ratio = lax.axis_size("row") // lax.axis_size("col")
    row_index = lax.axis_index("row")
    col_index = lax.axis_index("col")
    row_width = covariance.shape[0]
    tokens = lax.all_gather(context, "col", axis=0, tiled=True)
    partial_value = jnp.dot(tokens, weight, preferred_element_type=jnp.float32)
    summed = lax.psum_scatter(partial_value, "row", scatter_dimension=0, tiled=True)
    features = jnp.tanh(summed + feature_bias[None, :]).astype(jnp.bfloat16)
    phi_col = lax.all_gather(features, "row", axis=0, tiled=True)
    phi_held = broadcast(phi_col, "col", row_index // group_ratio)
    phi_row = lax.dynamic_slice_in_dim(phi_held, row_index % group_ratio * row_width, row_width, 1)
    col32 = phi_col.astype(jnp.float32)
    row32 = phi_row.astype(jnp.float32)
    panel_part = jnp.einsum("ik,bk->ib", covariance, col32, precision=highest)
    mean_part = jnp.dot(row32, prior_mean, precision=highest)
    panel = lax.psum(panel_part, "col")
    gram_part = jnp.dot(row32, panel, precision=highest)
    gram_matrix, predicted = lax.psum((gram_part, mean_part), "row")
    order = gram_matrix.shape[0]
    gram_matrix = gram_matrix + jnp.eye(order, dtype=jnp.float32)
    lower_factor = jnp.linalg.cholesky(gram_matrix)
    lower_inverse = lax.linalg.triangular_solve(
        lower_factor, jnp.eye(order, dtype=jnp.float32), left_side=True, lower=True
    )
    inverse_gram = jnp.dot(lower_inverse.T, lower_inverse, precision=highest)
    coeffs = jnp.dot(inverse_gram, rewards - predicted, precision=highest)
    gain_rows = jnp.dot(panel, inverse_gram, precision=highest)
    posterior_mean = prior_mean + jnp.dot(panel, coeffs, precision=highest)
    pieces = []
    for member in range(group_ratio):
        pieces.append(broadcast(panel, "row", col_index * group_ratio + member))
    far_panel = jnp.concatenate(pieces, 0)
    update = jnp.einsum("ib,jb->ij", gain_rows, far_panel, precision=highest)
    posterior_cov = covariance - update
    return (posterior_cov, posterior_mean)


def swap_col(x, step):
    n = lax.axis_size("col")
    return lax.ppermute(x, "col", [(i, i ^ step) for i in range(n)])


def swap_outer(x, step):
    n, inner = lax.axis_size("row"), lax.axis_size("row") // lax.axis_size("col")
    return lax.ppermute(x, "row", [(i, i ^ (step * inner)) for i in range(n)])


def swap_inner(x, step):
    return lax.ppermute(x, "row", [(i, i ^ step) for i in range(lax.axis_size("row"))])


def transpose(x):
    cols = lax.axis_size("col")
    inner = lax.axis_size("row") // cols
    pairs = []
    for outer in range(cols):
        for k in range(inner):
            for col in range(cols):
                pairs.append(((outer * inner + k) * cols + col, (col * inner + k) * cols + outer))
    return lax.ppermute(x, ("row", "col"), pairs)


def total(x):
    step = 1
    while step < lax.axis_size("row"):
        x = x + lax.ppermute(x, "row", [(i, i ^ step) for i in range(lax.axis_size("row"))])
        step *= 2
    step = 1
    while step < lax.axis_size("col"):
        x = x + swap_col(x, step)
        step *= 2
    return x


def places():
    cols = lax.axis_size("col")
    inner = lax.axis_size("row") // cols
    row = lax.axis_index("row")
    return row // inner, row % inner, lax.axis_index("col"), inner, cols


def span(index, size):
    return pl.ds(pl.multiple_of(index * size, size), size)


def call(kernel, name, limit, operands, in_specs, out_specs, out_shape, scratch_shapes=(), flops=0, size=0):
    return pl.pallas_call(
        kernel,
        in_specs=in_specs,
        out_specs=out_specs,
        out_shape=out_shape,
        scratch_shapes=scratch_shapes,
        cost_estimate=pl.CostEstimate(flops=flops, bytes_accessed=size, transcendentals=0),
        compiler_params=pltpu.CompilerParams(vmem_limit_bytes=limit * MIB),
        name=name,
    )(*operands)


def hold_kernel(in_ref, out_ref, sem):
    copy = pltpu.make_async_copy(in_ref, out_ref, sem)
    copy.start()
    copy.wait()


def hold(x, name):
    return call(
        hold_kernel,
        name,
        1,
        (x,),
        [pl.BlockSpec(memory_space=pl.ANY)],
        pl.BlockSpec(memory_space=pltpu.VMEM),
        pltpu.VMEM(x.shape, x.dtype),
        [pltpu.SemaphoreType.DMA],
        size=x.size * x.dtype.itemsize,
    )


def in_vmem(x):
    return pltpu.with_memory_space_constraint(x, pltpu.VMEM)


def preact_kernel(step, *refs):
    *blocks, w_ref, out_ref, held = refs
    _, inner_index, col, _, _ = places()
    rows = blocks[0].shape[0]
    width = out_ref.shape[1]
    tile = min(512, width)
    for s, block in enumerate(blocks):
        held[span(col ^ s, rows), :] = block[...].astype(F32)
    tokens = held[...].astype(BF16)
    first = (inner_index ^ step) * (width // tile)
    for t in range(width // tile):
        out_ref[:, t * tile : (t + 1) * tile] = dot(tokens, w_ref[:, span(first + t, tile)])


def preact_part(step, blocks, weight, width):
    rows, depth = blocks[0].shape
    n = len(blocks)
    return call(
        functools.partial(preact_kernel, step),
        "preact_part",
        8,
        (*blocks, in_vmem(weight)),
        vmem(n + 1),
        vmem(1)[0],
        jax.ShapeDtypeStruct((rows * n, width), F32),
        [pltpu.VMEM((rows * n, depth), F32)],
        2 * rows * n * depth * width,
        2 * depth * width,
    )


def scatter_kernel(n, *refs):
    sums, outs = refs[:n], refs[n:]
    outer, *_ = places()
    width = outs[0].shape[1]
    for s, out in enumerate(outs):
        here = span(outer ^ s, width)
        out[...] = sum(x[:, here] for x in sums)


def scatter(sums, count):
    rows, width = sums[0].shape
    shape = jax.ShapeDtypeStruct((rows, width // count), F32)
    return call(
        functools.partial(scatter_kernel, len(sums)), "scatter", 8, sums, vmem(len(sums)), vmem(count), [shape] * count, size=8 * rows * width
    )


def feature_kernel(bias_ref, *refs):
    *parts, out_ref = refs
    outer, inner_index, _, _, cols = places()
    here = span(inner_index * cols + outer, out_ref.shape[1])
    out_ref[...] = jnp.tanh(sum(p[...] for p in parts) + bias_ref[:, here]).astype(BF16)


def features_of(bias, parts):
    rows, width = parts[0].shape
    return call(
        feature_kernel,
        "features",
        8,
        (bias.reshape(1, bias.shape[0]), *parts),
        vmem(1 + len(parts)),
        vmem(1)[0],
        jax.ShapeDtypeStruct((rows, width), BF16),
        size=16 * rows * width,
    )


def panel_kernel(steps, last, c_ref, *refs):
    n = len(steps)
    shards, rest = refs[:n], refs[n:]
    outer, inner_index, col, _, cols = places()
    acc_ref = None if len(rest) == (cols if last else 1) else rest[0]
    outs = rest[-cols:] if last else rest[-1:]
    width = shards[0].shape[1]
    quarter = c_ref.shape[0] // cols
    rows = min(256, quarter)
    per = quarter // rows
    for q in range(cols):
        block = (col ^ q) if last else q

        @pl.loop(0, per)
        def _(i, q=q, block=block):
            here = span(block * per + i, rows)
            sums = None if acc_ref is None else acc_ref[here, :]
            for shard, (s, k) in zip(shards, steps):
                hi, lo = split2(c_ref[here, span((inner_index ^ k) * cols + (outer ^ s), width)])
                phi = shard[...]
                term = dot(hi, phi, NT) + dot(lo, phi, NT)
                sums = term if sums is None else sums + term
            if last:
                outs[q][span(i, rows), :] = sums.astype(outs[q].dtype)
            else:
                outs[0][here, :] = sums


def panel_part(covariance, shards, steps, acc=None, send=None):
    n = len(shards)
    batch, width = shards[0].shape
    rows = covariance.shape[0]
    cols = lax.axis_size("col")
    operands = [in_vmem(covariance), *shards] + ([] if acc is None else [acc])
    if send is None:
        shape = [jax.ShapeDtypeStruct((rows, batch), F32)]
    else:
        shape = [jax.ShapeDtypeStruct((rows // cols, batch), send if s else F32) for s in range(cols)]
    outs = call(
        functools.partial(panel_kernel, tuple(steps), send is not None),
        "panel_part",
        12,
        operands,
        vmem(len(operands)),
        vmem(len(shape)),
        shape,
        (),
        4 * rows * width * n * batch,
        4 * rows * width * n,
    )
    return outs[0] if send is None else outs


def gram_kernel(phi_ref, mean_ref, *refs):
    *parts, panel_ref, gram_ref = refs
    _, _, col, _, _ = places()
    panel = parts[0][...]
    for part in parts[1:]:
        panel = panel + part[...].astype(F32)
    panel_ref[...] = panel.astype(BF16)
    phi = phi_ref[...]
    batch = phi.shape[0]
    gram_ref[:batch, :] = sum(dot(phi, piece) for piece in split3(panel))
    mean = jnp.broadcast_to(mean_ref[:, span(col, panel.shape[0])], (8, panel.shape[0]))
    gram_ref[batch:, :] = sum(dot(piece, phi, NT) for piece in split3(mean))


def gram_part(phi, mean, parts):
    rows, batch = parts[0].shape
    return call(
        gram_kernel,
        "gram_part",
        8,
        (phi, mean.reshape(1, mean.shape[0]), *parts),
        vmem(2 + len(parts)),
        vmem(2),
        [jax.ShapeDtypeStruct((rows, batch), BF16), jax.ShapeDtypeStruct((batch + 8, batch), F32)],
    )


def inverse_kernel(gram_ref, rewards_ref, inverse_ref, coeffs_ref, held):
    n = rewards_ref.shape[1]
    highest = lax.Precision.HIGHEST
    lane = lax.broadcasted_iota(jnp.int32, (8, n), 1)
    sub = lax.broadcasted_iota(jnp.int32, (8, n), 0)
    i = lax.broadcasted_iota(jnp.int32, (n, n), 0)
    j = lax.broadcasted_iota(jnp.int32, (n, n), 1)
    held[...] = gram_ref[:n, :] + jnp.where(i == j, 1.0, 0.0)
    for first in range(0, n, 8):
        block = held[first : first + 8, :]
        inside = (lane >= first) & (lane < first + 8)
        eye = jnp.where(lane == sub + first, 1.0, 0.0)
        x, y = block, eye
        for t in range(8):
            column = jnp.broadcast_to(x[:, first + t : first + t + 1], (8, n))
            pivot = 1.0 / jnp.broadcast_to(x[t : t + 1, first + t : first + t + 1], (8, n))
            row_x = jnp.broadcast_to(x[t : t + 1, :], (8, n)) * pivot
            row_y = jnp.broadcast_to(y[t : t + 1, :], (8, n)) * pivot
            x = jnp.where(sub == t, row_x, x - column * row_x)
            y = jnp.where(sub == t, row_y, y - column * row_y)
        spread = jnp.where(inside, -y, x)
        rest = jnp.where((j >= first) & (j < first + 8), 0.0, held[...])
        held[...] = rest - lax.dot_general(block, spread, TN, precision=highest, preferred_element_type=F32)
        held[first : first + 8, :] = spread
    inverse = -held[...]
    inverse_ref[...] = inverse
    gap = jnp.broadcast_to(rewards_ref[...] - gram_ref[n : n + 1, :], (8, n))
    coeffs_ref[...] = lax.dot_general(gap, inverse, (((1,), (0,)), ((), ())), precision=highest, preferred_element_type=F32)


def inverse_and_coeffs(gram, rewards):
    n = rewards.shape[0]
    return call(
        inverse_kernel,
        "inverse",
        8,
        (gram, rewards.reshape(1, n)),
        vmem(2),
        vmem(2),
        [jax.ShapeDtypeStruct((n, n), F32), jax.ShapeDtypeStruct((8, n), F32)],
        [pltpu.VMEM((n, n), F32)],
    )


def update_kernel(near, far, tile, *refs):
    c_ref, inverse_ref, coeffs_ref, mean_ref = refs[:4]
    near_refs = refs[4 : 4 + near]
    far_refs = refs[4 + near : 4 + near + far]
    out_ref, new_mean_ref, gain, panel, other = refs[4 + near + far :]
    outer, inner_index, col, _, cols = places()
    batch = inverse_ref.shape[0]
    quarter = near_refs[0].shape[0]
    for s, part in enumerate(near_refs):
        panel[span(col ^ s, quarter), :] = part[...]
    for s, part in enumerate(far_refs):
        here = span((inner_index ^ (s // cols)) * cols + (outer ^ (s % cols)), quarter)
        other[here, :batch] = part[...]
        other[here, batch:] = part[...]
    hi, lo = split2(inverse_ref[...])
    rows = panel[...]
    product = dot(rows, hi) + dot(rows, lo)
    hi, lo = split2(product)
    gain[:, :batch] = hi
    gain[:, batch:] = lo
    new_mean_ref[...] = mean_ref[...] + sum(dot(p, rows, NT) for p in split3(coeffs_ref[...]))[:1]

    def body(step, block):
        here = span(step.index[0], tile)
        block[...] = c_ref[here, :] - dot(gain[here, :], other[...], NT)

    pltpu.emit_pipeline(
        body,
        grid=(c_ref.shape[0] // tile,),
        in_specs=[],
        out_specs=[pl.BlockSpec((tile, c_ref.shape[1]), lambda i: (i, 0))],
        _explicit_indices=True,
    )(out_ref)


def update(covariance, inverse, coeffs, mean, near, far):
    rows, cols = covariance.shape
    batch = inverse.shape[0]
    return call(
        functools.partial(update_kernel, len(near), len(far), min(256, rows)),
        "update",
        20,
        (in_vmem(covariance), inverse, coeffs, mean.reshape(1, rows), *near, *far),
        vmem(4 + len(near) + len(far)),
        [pl.BlockSpec(memory_space=pl.ANY), vmem(1)[0]],
        [jax.ShapeDtypeStruct((rows, cols), F32), jax.ShapeDtypeStruct((1, rows), F32)],
        [
            pltpu.VMEM((rows, 2 * batch), BF16),
            pltpu.VMEM((rows, batch), BF16),
            pltpu.VMEM((cols, 2 * batch), BF16),
        ],
    )


def per_device(context, weight, feature_bias, covariance, prior_mean, rewards):
    cols = lax.axis_size("col")
    inner = lax.axis_size("row") // cols
    rows, block = covariance.shape
    part = block // inner
    if (part // cols) % 128 or (rows // cols) % 128:
        return plain(context, weight, feature_bias, covariance, prior_mean, rewards)

    blocks = [context] + [swap_col(context, s) for s in range(1, cols)]
    w_held = hold(weight, "hold_weight")
    sums = []
    for k in range(inner - 1, -1, -1):
        piece = preact_part(k, blocks, w_held, part)
        sums.append(swap_inner(piece, k) if k else piece)
    pieces = scatter(sums, cols)
    summed = [pieces[0]] + [swap_outer(pieces[s], s) for s in range(1, cols)]
    features = features_of(feature_bias, summed)

    held = hold(covariance, "hold_covariance")
    shards = [features] + [swap_outer(features, s) for s in range(1, cols)]
    panel = panel_part(held, shards, [(s, 0) for s in range(cols)])
    for k in range(1, inner):
        others = [swap_inner(s, k) for s in shards]
        panel = panel_part(
            held, others, [(s, k) for s in range(cols)], panel, F32 if k == inner - 1 else None
        )

    far_features = transpose(features)
    parts = [panel[0]] + [swap_col(panel[s], s) for s in range(1, cols)]
    own_panel, gram = gram_part(far_features, prior_mean, parts)
    near = [own_panel] + [swap_col(own_panel, s) for s in range(1, cols)]
    turned = transpose(own_panel)
    far = [turned] + [swap_outer(turned, s) for s in range(1, cols)]
    for k in range(1, inner):
        far += [swap_inner(f, k) for f in far[:cols]]

    inverse, coeffs = inverse_and_coeffs(total(gram), rewards)
    new_cov, new_mean = update(held, inverse, coeffs, prior_mean, near, far)
    return new_cov, new_mean.reshape(rows)


def solution(mesh):
    return jax.shard_map(
        per_device,
        mesh=mesh,
        in_specs=(P("col", "row"), P("row", "col"), P("col"), P("row", "col"), P("row"), P()),
        out_specs=(P("row", "col"), P("row")),
        check_vma=False,
    )
```

```python
import functools

import jax
import jax.numpy as jnp
from jax import lax
from jax.experimental import pallas as pl
from jax.experimental.pallas import tpu as pltpu
from jax.sharding import PartitionSpec as P

F32 = jnp.float32
BF16 = jnp.bfloat16
MIB = 1 << 20
NT = (((1,), (1,)), ((), ()))
TN = (((0,), (0,)), ((), ()))


def dot(a, b, dims=(((1,), (0,)), ((), ()))):
    return lax.dot_general(a, b, dims, preferred_element_type=F32)


def split2(x):
    hi = x.astype(BF16)
    return hi, (x - hi.astype(F32)).astype(BF16)


def split3(x):
    hi = x.astype(BF16)
    rest = x - hi.astype(F32)
    mid = rest.astype(BF16)
    return hi, mid, (rest - mid.astype(F32)).astype(BF16)


def vmem(n):
    return [pl.BlockSpec(memory_space=pltpu.VMEM)] * n


def broadcast(array, axis, root):
    mine = lax.axis_index(axis) == root
    return lax.psum(jnp.where(mine, array, jnp.zeros_like(array)), axis)


def plain(context, weight, feature_bias, covariance, prior_mean, rewards):
    highest = lax.Precision.HIGHEST
    group_ratio = lax.axis_size("row") // lax.axis_size("col")
    row_index = lax.axis_index("row")
    col_index = lax.axis_index("col")
    row_width = covariance.shape[0]
    tokens = lax.all_gather(context, "col", axis=0, tiled=True)
    partial_value = jnp.dot(tokens, weight, preferred_element_type=jnp.float32)
    summed = lax.psum_scatter(partial_value, "row", scatter_dimension=0, tiled=True)
    features = jnp.tanh(summed + feature_bias[None, :]).astype(jnp.bfloat16)
    phi_col = lax.all_gather(features, "row", axis=0, tiled=True)
    phi_held = broadcast(phi_col, "col", row_index // group_ratio)
    phi_row = lax.dynamic_slice_in_dim(phi_held, row_index % group_ratio * row_width, row_width, 1)
    col32 = phi_col.astype(jnp.float32)
    row32 = phi_row.astype(jnp.float32)
    panel_part = jnp.einsum("ik,bk->ib", covariance, col32, precision=highest)
    mean_part = jnp.dot(row32, prior_mean, precision=highest)
    panel = lax.psum(panel_part, "col")
    gram_part = jnp.dot(row32, panel, precision=highest)
    gram_matrix, predicted = lax.psum((gram_part, mean_part), "row")
    order = gram_matrix.shape[0]
    gram_matrix = gram_matrix + jnp.eye(order, dtype=jnp.float32)
    lower_factor = jnp.linalg.cholesky(gram_matrix)
    lower_inverse = lax.linalg.triangular_solve(
        lower_factor, jnp.eye(order, dtype=jnp.float32), left_side=True, lower=True
    )
    inverse_gram = jnp.dot(lower_inverse.T, lower_inverse, precision=highest)
    coeffs = jnp.dot(inverse_gram, rewards - predicted, precision=highest)
    gain_rows = jnp.dot(panel, inverse_gram, precision=highest)
    posterior_mean = prior_mean + jnp.dot(panel, coeffs, precision=highest)
    pieces = []
    for member in range(group_ratio):
        pieces.append(broadcast(panel, "row", col_index * group_ratio + member))
    far_panel = jnp.concatenate(pieces, 0)
    update = jnp.einsum("ib,jb->ij", gain_rows, far_panel, precision=highest)
    posterior_cov = covariance - update
    return (posterior_cov, posterior_mean)


def swap_col(x, step):
    n = lax.axis_size("col")
    return lax.ppermute(x, "col", [(i, i ^ step) for i in range(n)])


def swap_outer(x, step):
    n, inner = lax.axis_size("row"), lax.axis_size("row") // lax.axis_size("col")
    return lax.ppermute(x, "row", [(i, i ^ (step * inner)) for i in range(n)])


def swap_inner(x, step):
    return lax.ppermute(x, "row", [(i, i ^ step) for i in range(lax.axis_size("row"))])


def transpose(x):
    cols = lax.axis_size("col")
    inner = lax.axis_size("row") // cols
    pairs = []
    for outer in range(cols):
        for k in range(inner):
            for col in range(cols):
                pairs.append(((outer * inner + k) * cols + col, (col * inner + k) * cols + outer))
    return lax.ppermute(x, ("row", "col"), pairs)


def places():
    cols = lax.axis_size("col")
    inner = lax.axis_size("row") // cols
    row = lax.axis_index("row")
    return row // inner, row % inner, lax.axis_index("col"), inner, cols


def span(index, size):
    return pl.ds(pl.multiple_of(index * size, size), size)


def call(kernel, name, operands, in_specs, out_specs, out_shape, scratch_shapes=(), flops=0, size=0):
    return pl.pallas_call(
        kernel,
        in_specs=in_specs,
        out_specs=out_specs,
        out_shape=out_shape,
        scratch_shapes=scratch_shapes,
        cost_estimate=pl.CostEstimate(flops=flops, bytes_accessed=size, transcendentals=0),
        compiler_params=pltpu.CompilerParams(vmem_limit_bytes=14 * MIB),
        name=name,
    )(*operands)


def hold_kernel(in_ref, *refs):
    out_ref, token_ref, sem = refs[-3:]
    copy = pltpu.make_async_copy(in_ref, out_ref, sem)
    copy.start()
    token_ref[...] = jnp.zeros_like(token_ref)
    copy.wait()


def hold(x, name, *after):
    return call(
        hold_kernel,
        name,
        (x, *after),
        [pl.BlockSpec(memory_space=pl.ANY)] * (1 + len(after)),
        vmem(2),
        [pltpu.VMEM(x.shape, x.dtype), jax.ShapeDtypeStruct((8, 128), F32)],
        [pltpu.SemaphoreType.DMA],
        size=x.size * x.dtype.itemsize,
    )


def in_vmem(x):
    return pltpu.with_memory_space_constraint(x, pltpu.VMEM)


def preact_kernel(step, *refs):
    *blocks, w_ref, out_ref, held = refs
    _, inner_index, col, _, _ = places()
    rows = blocks[0].shape[0]
    width = out_ref.shape[1]
    tile = min(512, width)
    for s, block in enumerate(blocks):
        held[span(col ^ s, rows), :] = block[...].astype(F32)
    tokens = held[...].astype(BF16)
    first = (inner_index ^ step) * (width // tile)
    for t in range(width // tile):
        out_ref[:, t * tile : (t + 1) * tile] = dot(tokens, w_ref[:, span(first + t, tile)])


def preact_part(step, blocks, weight, width):
    rows, depth = blocks[0].shape
    n = len(blocks)
    return call(
        functools.partial(preact_kernel, step),
        "preact_part",
        (*blocks, in_vmem(weight)),
        vmem(n + 1),
        vmem(1)[0],
        jax.ShapeDtypeStruct((rows * n, width), F32),
        [pltpu.VMEM((rows * n, depth), F32)],
        2 * rows * n * depth * width,
        2 * depth * width,
    )


def scatter_kernel(n, *refs):
    sums, outs = refs[:n], refs[n:]
    outer, *_ = places()
    width = outs[0].shape[1]
    for s, out in enumerate(outs):
        here = span(outer ^ s, width)
        out[...] = sum(x[:, here] for x in sums)


def scatter(sums, count):
    rows, width = sums[0].shape
    shape = jax.ShapeDtypeStruct((rows, width // count), F32)
    return call(
        functools.partial(scatter_kernel, len(sums)), "scatter", sums, vmem(len(sums)), vmem(count), [shape] * count, size=8 * rows * width
    )


def feature_kernel(_, bias_ref, *refs):
    *parts, out_ref = refs
    outer, inner_index, _, _, cols = places()
    here = span(inner_index * cols + outer, out_ref.shape[1])
    out_ref[...] = jnp.tanh(sum(p[...] for p in parts) + bias_ref[:, here]).astype(BF16)


def features_of(token, bias, parts):
    rows, width = parts[0].shape
    return call(
        feature_kernel,
        "features",
        (token, bias.reshape(1, bias.shape[0]), *parts),
        vmem(2 + len(parts)),
        vmem(1)[0],
        jax.ShapeDtypeStruct((rows, width), BF16),
        size=16 * rows * width,
    )


def panel_kernel(steps, last, c_ref, *refs):
    n = len(steps)
    shards, rest = refs[:n], refs[n:]
    outer, inner_index, col, _, cols = places()
    acc_ref = None if len(rest) == (cols if last else 1) else rest[0]
    outs = rest[-cols:] if last else rest[-1:]
    width = shards[0].shape[1]
    quarter = c_ref.shape[0] // cols
    rows = min(512, quarter)
    per = quarter // rows
    for q in range(cols):
        block = (col ^ q) if last else q

        @pl.loop(0, per)
        def _(i, q=q, block=block):
            here = span(block * per + i, rows)
            sums = None if acc_ref is None else acc_ref[here, :]
            for shard, (s, k) in zip(shards, steps):
                hi, lo = split2(c_ref[here, span((inner_index ^ k) * cols + (outer ^ s), width)])
                phi = shard[...]
                term = dot(hi, phi, NT) + dot(lo, phi, NT)
                sums = term if sums is None else sums + term
            if last:
                outs[q][span(i, rows), :] = sums.astype(outs[q].dtype)
            else:
                outs[0][here, :] = sums


def panel_part(covariance, shards, steps, acc=None, send=None):
    n = len(shards)
    batch, width = shards[0].shape
    rows = covariance.shape[0]
    cols = lax.axis_size("col")
    operands = [in_vmem(covariance), *shards] + ([] if acc is None else [acc])
    if send is None:
        shape = [jax.ShapeDtypeStruct((rows, batch), F32)]
    else:
        shape = [jax.ShapeDtypeStruct((rows // cols, batch), send if s else F32) for s in range(cols)]
    outs = call(
        functools.partial(panel_kernel, tuple(steps), send is not None),
        "panel_part",
        operands,
        vmem(len(operands)),
        vmem(len(shape)),
        shape,
        (),
        4 * rows * width * n * batch,
        4 * rows * width * n,
    )
    return outs[0] if send is None else outs


def gram_kernel(_, phi_ref, mean_ref, *refs):
    *parts, panel_ref, gram_ref = refs
    _, _, col, _, _ = places()
    panel = parts[0][...]
    for part in parts[1:]:
        panel = panel + part[...].astype(F32)
    panel_ref[...] = panel.astype(BF16)
    phi = phi_ref[...]
    batch = phi.shape[0]
    gram_ref[:batch, :] = sum(dot(phi, piece) for piece in split3(panel))
    mean = jnp.broadcast_to(mean_ref[:, span(col, panel.shape[0])], (8, panel.shape[0]))
    gram_ref[batch:, :] = sum(dot(piece, phi, NT) for piece in split3(mean))


def gram_part(held, phi, mean, parts):
    rows, batch = parts[0].shape
    return call(
        gram_kernel,
        "gram_part",
        (in_vmem(held), phi, mean.reshape(1, mean.shape[0]), *parts),
        vmem(3 + len(parts)),
        vmem(2),
        [jax.ShapeDtypeStruct((rows, batch), BF16), jax.ShapeDtypeStruct((batch + 8, batch), F32)],
    )


def join_kernel(count, _, x_ref, y_ref, *refs):
    out_ref = refs[count]
    out_ref[...] = x_ref[...] + y_ref[...]
    for source, target in zip(refs[:count], refs[count + 1 :]):
        target[...] = source[...]


def join(held, x, y, *others):
    outs = call(
        functools.partial(join_kernel, len(others)),
        "join",
        (in_vmem(held), x, y, *others),
        vmem(3 + len(others)),
        vmem(1 + len(others)),
        [jax.ShapeDtypeStruct(a.shape, a.dtype) for a in (x, *others)],
    )
    return outs if others else outs[0]


def total_row(held, x, *others):
    step, size = 1, lax.axis_size("row")
    while step < size:
        y = lax.ppermute(x, "row", [(i, i ^ step) for i in range(size)])
        step *= 2
        if step == size and others:
            return join(held, x, y, *others)
        x = join(held, x, y)
    return x


def total_col(held, x, *others):
    step, size = 1, lax.axis_size("col")
    while step < size:
        y = swap_col(x, step)
        step *= 2
        if step == size and others:
            return join(held, x, y, *others)
        x = join(held, x, y)
    return x


def inverse_kernel(_, gram_ref, rewards_ref, inverse_ref, coeffs_ref):
    n = rewards_ref.shape[1]
    lane = lax.broadcasted_iota(jnp.int32, (8, n), 1)
    sub = lax.broadcasted_iota(jnp.int32, (8, n), 0)

    def row(x, t):
        return jnp.broadcast_to(x[t : t + 1, :], (8, n))

    def column(x, t):
        return jnp.broadcast_to(x[:, t : t + 1], (8, n))

    groups = [
        gram_ref[first : first + 8, :] + jnp.where(lane == sub + first, 1.0, 0.0) for first in range(0, n, 8)
    ]
    for g in range(n // 8):
        first = 8 * g
        inside = (lane >= first) & (lane < first + 8)
        eye = jnp.where(lane == sub + first, 1.0, 0.0)
        columns = [column(groups[g], first + t) for t in range(8)]
        swept = jnp.where(inside, eye, groups[g])
        for t in range(8):
            scale = 1.0 / row(columns[t], t)
            factor = columns[t]

            def eliminate(x):
                mine = row(x, t) * scale
                return jnp.where(sub == t, mine, x - factor * mine)

            swept = eliminate(swept)
            for u in range(t + 1, 8):
                columns[u] = eliminate(columns[u])
        swept = jnp.where(inside, -swept, swept)
        rows = [row(swept, t) for t in range(8)]
        order = [h % (n // 8) for h in range(g + 1, g + n // 8)]
        for h in order:
            x = jnp.where(inside, 0.0, groups[h])
            for t in range(8):
                x = x - column(groups[h], first + t) * rows[t]
            groups[h] = x
        groups[g] = swept
    for g in range(n // 8):
        inverse_ref[8 * g : 8 * g + 8, :] = -groups[g]
    gap = jnp.broadcast_to(rewards_ref[...] - gram_ref[n : n + 1, :], (8, n))
    coeffs_ref[...] = lax.dot_general(
        gap,
        inverse_ref[...],
        (((1,), (0,)), ((), ())),
        precision=lax.Precision.HIGHEST,
        preferred_element_type=F32,
    )


def inverse_and_coeffs(held, gram, rewards):
    n = rewards.shape[0]
    return call(
        inverse_kernel,
        "inverse",
        (in_vmem(held), gram, rewards.reshape(1, n)),
        vmem(3),
        vmem(2),
        [jax.ShapeDtypeStruct((n, n), F32), jax.ShapeDtypeStruct((8, n), F32)],
    )


def update_kernel(near, far, tile, *refs):
    c_ref, inverse_ref, coeffs_ref, mean_ref = refs[:4]
    near_refs = refs[4 : 4 + near]
    far_refs = refs[4 + near : 4 + near + far]
    out_ref, new_mean_ref, gain, panel, other = refs[4 + near + far :]
    outer, inner_index, col, _, cols = places()
    batch = inverse_ref.shape[0]
    quarter = near_refs[0].shape[0]
    for s, part in enumerate(near_refs):
        panel[span(col ^ s, quarter), :] = part[...]
    for s, part in enumerate(far_refs):
        here = span((inner_index ^ (s // cols)) * cols + (outer ^ (s % cols)), quarter)
        other[here, :batch] = part[...]
        other[here, batch:] = part[...]
    hi, lo = split2(inverse_ref[...])
    rows = panel[...]
    product = dot(rows, hi) + dot(rows, lo)
    hi, lo = split2(product)
    gain[:, :batch] = hi
    gain[:, batch:] = lo
    new_mean_ref[...] = mean_ref[...] + sum(dot(p, rows, NT) for p in split3(coeffs_ref[...]))[:1]

    def body(step, block):
        here = span(step.index[0], tile)
        block[...] = c_ref[:, here] - dot(gain[...], other[here, :], NT)

    pltpu.emit_pipeline(
        body,
        grid=(c_ref.shape[1] // tile,),
        in_specs=[],
        out_specs=[pl.BlockSpec((c_ref.shape[0], tile), lambda i: (0, i))],
        _explicit_indices=True,
    )(out_ref)


def update(covariance, inverse, coeffs, mean, near, far):
    rows, cols = covariance.shape
    batch = inverse.shape[0]
    return call(
        functools.partial(update_kernel, len(near), len(far), min(256, cols)),
        "update",
        (in_vmem(covariance), inverse, coeffs, mean.reshape(1, rows), *near, *far),
        vmem(4 + len(near) + len(far)),
        [pl.BlockSpec(memory_space=pl.ANY), vmem(1)[0]],
        [jax.ShapeDtypeStruct((rows, cols), F32), jax.ShapeDtypeStruct((1, rows), F32)],
        [
            pltpu.VMEM((rows, 2 * batch), BF16),
            pltpu.VMEM((rows, batch), BF16),
            pltpu.VMEM((cols, 2 * batch), BF16),
        ],
    )


def per_device(context, weight, feature_bias, covariance, prior_mean, rewards):
    cols = lax.axis_size("col")
    inner = lax.axis_size("row") // cols
    rows, block = covariance.shape
    part = block // inner
    if (part // cols) % 128 or (rows // cols) % 128:
        return plain(context, weight, feature_bias, covariance, prior_mean, rewards)

    blocks = [context] + [swap_col(context, s) for s in range(1, cols)]
    w_held, _ = hold(weight, "hold_weight")
    sums = []
    for k in range(inner - 1, -1, -1):
        piece = preact_part(k, blocks, w_held, part)
        sums.append(swap_inner(piece, k) if k else piece)
    pieces = scatter(sums, cols)
    summed = [pieces[0]] + [swap_outer(pieces[s], s) for s in range(1, cols)]
    held, token = hold(covariance, "hold_covariance", pieces[0])
    features = features_of(token, feature_bias, summed)

    shards = [features] + [swap_outer(features, s) for s in range(1, cols)]
    panel = panel_part(held, shards[:1], [(0, 0)])
    panel = panel_part(held, shards[1:], [(s, 0) for s in range(1, cols)], panel)
    for k in range(1, inner):
        others = [swap_inner(s, k) for s in shards]
        panel = panel_part(held, others, [(s, k) for s in range(cols)], panel, F32 if k == inner - 1 else None)

    far_features = transpose(features)
    parts = [panel[0]] + [swap_col(panel[s], s) for s in range(1, cols)]
    own_panel, gram = gram_part(held, far_features, prior_mean, parts)
    gram, turned = total_row(held, gram, transpose(own_panel))
    far = [turned] + [swap_outer(turned, s) for s in range(1, cols)]
    gram, own_panel = total_col(held, gram, own_panel)
    near = [own_panel] + [swap_col(own_panel, s) for s in range(1, cols)]
    for k in range(1, inner):
        far += [swap_inner(f, k) for f in far[:cols]]

    inverse, coeffs = inverse_and_coeffs(held, gram, rewards)
    new_cov, new_mean = update(held, inverse, coeffs, prior_mean, near, far)
    return new_cov, new_mean.reshape(rows)


def solution(mesh):
    return jax.shard_map(
        per_device,
        mesh=mesh,
        in_specs=(P("col", "row"), P("row", "col"), P("col"), P("row", "col"), P("row"), P()),
        out_specs=(P("row", "col"), P("row")),
        check_vma=False,
    )
```

```python
import functools

import jax
import jax.numpy as jnp
from jax import lax
from jax.experimental import pallas as pl
from jax.experimental.pallas import tpu as pltpu
from jax.sharding import PartitionSpec as P

F32 = jnp.float32
BF16 = jnp.bfloat16
MIB = 1 << 20
NT = (((1,), (1,)), ((), ()))
TN = (((0,), (0,)), ((), ()))


def dot(a, b, dims=(((1,), (0,)), ((), ()))):
    return lax.dot_general(a, b, dims, preferred_element_type=F32)


def split2(x):
    hi = x.astype(BF16)
    return hi, (x - hi.astype(F32)).astype(BF16)


def split3(x):
    hi = x.astype(BF16)
    rest = x - hi.astype(F32)
    mid = rest.astype(BF16)
    return hi, mid, (rest - mid.astype(F32)).astype(BF16)


def vmem(n):
    return [pl.BlockSpec(memory_space=pltpu.VMEM)] * n


def broadcast(array, axis, root):
    mine = lax.axis_index(axis) == root
    return lax.psum(jnp.where(mine, array, jnp.zeros_like(array)), axis)


def plain(context, weight, feature_bias, covariance, prior_mean, rewards):
    highest = lax.Precision.HIGHEST
    group_ratio = lax.axis_size("row") // lax.axis_size("col")
    row_index = lax.axis_index("row")
    col_index = lax.axis_index("col")
    row_width = covariance.shape[0]
    tokens = lax.all_gather(context, "col", axis=0, tiled=True)
    partial_value = jnp.dot(tokens, weight, preferred_element_type=jnp.float32)
    summed = lax.psum_scatter(partial_value, "row", scatter_dimension=0, tiled=True)
    features = jnp.tanh(summed + feature_bias[None, :]).astype(jnp.bfloat16)
    phi_col = lax.all_gather(features, "row", axis=0, tiled=True)
    phi_held = broadcast(phi_col, "col", row_index // group_ratio)
    phi_row = lax.dynamic_slice_in_dim(phi_held, row_index % group_ratio * row_width, row_width, 1)
    col32 = phi_col.astype(jnp.float32)
    row32 = phi_row.astype(jnp.float32)
    panel_part = jnp.einsum("ik,bk->ib", covariance, col32, precision=highest)
    mean_part = jnp.dot(row32, prior_mean, precision=highest)
    panel = lax.psum(panel_part, "col")
    gram_part = jnp.dot(row32, panel, precision=highest)
    gram_matrix, predicted = lax.psum((gram_part, mean_part), "row")
    order = gram_matrix.shape[0]
    gram_matrix = gram_matrix + jnp.eye(order, dtype=jnp.float32)
    lower_factor = jnp.linalg.cholesky(gram_matrix)
    lower_inverse = lax.linalg.triangular_solve(
        lower_factor, jnp.eye(order, dtype=jnp.float32), left_side=True, lower=True
    )
    inverse_gram = jnp.dot(lower_inverse.T, lower_inverse, precision=highest)
    coeffs = jnp.dot(inverse_gram, rewards - predicted, precision=highest)
    gain_rows = jnp.dot(panel, inverse_gram, precision=highest)
    posterior_mean = prior_mean + jnp.dot(panel, coeffs, precision=highest)
    pieces = []
    for member in range(group_ratio):
        pieces.append(broadcast(panel, "row", col_index * group_ratio + member))
    far_panel = jnp.concatenate(pieces, 0)
    update = jnp.einsum("ib,jb->ij", gain_rows, far_panel, precision=highest)
    posterior_cov = covariance - update
    return (posterior_cov, posterior_mean)


def swap_col(x, step):
    n = lax.axis_size("col")
    return lax.ppermute(x, "col", [(i, i ^ step) for i in range(n)])


def swap_outer(x, step):
    n, inner = lax.axis_size("row"), lax.axis_size("row") // lax.axis_size("col")
    return lax.ppermute(x, "row", [(i, i ^ (step * inner)) for i in range(n)])


def swap_inner(x, step):
    return lax.ppermute(x, "row", [(i, i ^ step) for i in range(lax.axis_size("row"))])


def transpose(x, step=0):
    cols = lax.axis_size("col")
    inner = lax.axis_size("row") // cols
    pairs = []
    for outer in range(cols):
        for k in range(inner):
            for col in range(cols):
                pairs.append(((outer * inner + k) * cols + col, ((col ^ step) * inner + k) * cols + outer))
    return lax.ppermute(x, ("row", "col"), pairs)


def places():
    cols = lax.axis_size("col")
    inner = lax.axis_size("row") // cols
    row = lax.axis_index("row")
    return row // inner, row % inner, lax.axis_index("col"), inner, cols


def span(index, size):
    return pl.ds(pl.multiple_of(index * size, size), size)


def call(kernel, name, operands, in_specs, out_specs, out_shape, scratch_shapes=(), flops=0, size=0):
    return pl.pallas_call(
        kernel,
        in_specs=in_specs,
        out_specs=out_specs,
        out_shape=out_shape,
        scratch_shapes=scratch_shapes,
        cost_estimate=pl.CostEstimate(flops=flops, bytes_accessed=size, transcendentals=0),
        compiler_params=pltpu.CompilerParams(vmem_limit_bytes=14 * MIB),
        name=name,
    )(*operands)


def hold_kernel(*refs):
    n = len(refs) // 2
    copies = [pltpu.make_async_copy(refs[i], refs[n + i], refs[-1].at[i]) for i in range(n)]
    for copy in copies:
        copy.start()
    for copy in copies:
        copy.wait()


def hold(*arrays):
    return call(
        hold_kernel,
        "hold_weight",
        [in_hbm(x) for x in arrays],
        [pl.BlockSpec(memory_space=pl.ANY)] * len(arrays),
        vmem(len(arrays)),
        [pltpu.VMEM(x.shape, x.dtype) for x in arrays[:1]]
        + [jax.ShapeDtypeStruct(x.shape, x.dtype) for x in arrays[1:]],
        [pltpu.SemaphoreType.DMA((len(arrays),))],
        size=arrays[0].size * arrays[0].dtype.itemsize,
    )


def touch_kernel(*refs):
    refs[-1][...] = jnp.zeros_like(refs[-1])


def touch(x, *after):
    return call(
        touch_kernel,
        "touch",
        (in_vmem(x), *after),
        vmem(1) + [pl.BlockSpec(memory_space=pl.ANY)] * len(after),
        vmem(1)[0],
        jax.ShapeDtypeStruct((8, 128), F32),
    )


def in_hbm(x):
    return pltpu.with_memory_space_constraint(x, pltpu.HBM)


def in_vmem(x):
    return pltpu.with_memory_space_constraint(x, pltpu.VMEM)


def preact_kernel(step, *refs):
    *blocks, w_ref, out_ref, held = refs
    _, inner_index, col, _, _ = places()
    rows = blocks[0].shape[0]
    width = out_ref.shape[1]
    tile = min(512, width)
    for s, block in enumerate(blocks):
        held[span(col ^ s, rows), :] = block[...].astype(F32)
    tokens = held[...].astype(BF16)
    first = (inner_index ^ step) * (width // tile)
    for t in range(width // tile):
        out_ref[:, t * tile : (t + 1) * tile] = dot(tokens, w_ref[:, span(first + t, tile)])


def preact_part(step, blocks, weight, width):
    rows, depth = blocks[0].shape
    n = len(blocks)
    return call(
        functools.partial(preact_kernel, step),
        "preact_part",
        (*blocks, in_vmem(weight)),
        vmem(n + 1),
        vmem(1)[0],
        jax.ShapeDtypeStruct((rows * n, width), F32),
        [pltpu.VMEM((rows * n, depth), F32)],
        2 * rows * n * depth * width,
        2 * depth * width,
    )


def scatter_kernel(n, *refs):
    sums, outs = refs[:n], refs[n:]
    outer, *_ = places()
    width = outs[0].shape[1]
    for s, out in enumerate(outs):
        here = span(outer ^ s, width)
        out[...] = sum(x[:, here] for x in sums)


def scatter(sums, count):
    rows, width = sums[0].shape
    shape = jax.ShapeDtypeStruct((rows, width // count), F32)
    return call(
        functools.partial(scatter_kernel, len(sums)), "scatter", sums, vmem(len(sums)), vmem(count), [shape] * count, size=8 * rows * width
    )


def feature_kernel(_, bias_ref, *refs):
    *parts, out_ref = refs
    outer, inner_index, _, _, cols = places()
    here = span(inner_index * cols + outer, out_ref.shape[1])
    out_ref[...] = jnp.tanh(sum(p[...] for p in parts) + bias_ref[:, here]).astype(BF16)


def features_of(token, bias, parts):
    rows, width = parts[0].shape
    return call(
        feature_kernel,
        "features",
        (token, bias, *parts),
        vmem(2 + len(parts)),
        vmem(1)[0],
        jax.ShapeDtypeStruct((rows, width), BF16),
        size=16 * rows * width,
    )


def panel_kernel(steps, kind, c_ref, *refs):
    n = len(steps)
    last = kind == "last"
    shards, rest = refs[:n], refs[n:]
    outer, inner_index, col, _, cols = places()
    acc_ref = None if kind == "first" else rest[0]
    outs = rest[0 if acc_ref is None else 1 :]
    if kind == "first":
        outs[1][...] = shards[0][...]
    width = shards[0].shape[1]
    quarter = c_ref.shape[0] // cols
    rows = min(512, quarter)
    per = quarter // rows
    for q in range(cols):
        block = (col ^ q) if last else q

        @pl.loop(0, per)
        def _(i, q=q, block=block):
            here = span(block * per + i, rows)
            sums = None if acc_ref is None else acc_ref[here, :]
            for shard, (s, k) in zip(shards, steps):
                hi, lo = split2(c_ref[here, span((inner_index ^ k) * cols + (outer ^ s), width)])
                phi = shard[...]
                term = dot(hi, phi, NT) + dot(lo, phi, NT)
                sums = term if sums is None else sums + term
            if last:
                outs[q][span(i, rows), :] = sums.astype(outs[q].dtype)
            else:
                outs[0][here, :] = sums


def panel_part(covariance, shards, steps, kind, acc=None):
    n = len(shards)
    batch, width = shards[0].shape
    rows = covariance.shape[0]
    cols = lax.axis_size("col")
    operands = [in_vmem(covariance), *shards] + ([] if acc is None else [acc])
    shape = [jax.ShapeDtypeStruct((rows, batch), F32)]
    if kind == "last":
        shape = [jax.ShapeDtypeStruct((rows // cols, batch), F32)] * cols
    if kind == "first":
        shape.append(jax.ShapeDtypeStruct((batch, width), BF16))
    outs = call(
        functools.partial(panel_kernel, tuple(steps), kind),
        "panel_part",
        operands,
        vmem(len(operands)),
        vmem(len(shape)),
        shape,
        (),
        4 * rows * width * n * batch,
        4 * rows * width * n,
    )
    return outs if len(shape) > 1 else outs[0]


def gram_kernel(_, phi_ref, mean_ref, *refs):
    *parts, panel_ref, gram_ref = refs
    _, _, col, _, _ = places()
    panel = parts[0][...]
    for part in parts[1:]:
        panel = panel + part[...].astype(F32)
    panel_ref[...] = panel.astype(BF16)
    phi = phi_ref[...]
    batch = phi.shape[0]
    gram_ref[:batch, :] = sum(dot(phi, piece) for piece in split3(panel))
    mean = jnp.broadcast_to(mean_ref[:, span(col, panel.shape[0])], (8, panel.shape[0]))
    gram_ref[batch:, :] = sum(dot(piece, phi, NT) for piece in split3(mean))


def gram_part(held, phi, mean, parts):
    rows, batch = parts[0].shape
    return call(
        gram_kernel,
        "gram_part",
        (in_vmem(held), phi, mean.reshape(1, mean.shape[0]), *parts),
        vmem(3 + len(parts)),
        vmem(2),
        [jax.ShapeDtypeStruct((rows, batch), BF16), jax.ShapeDtypeStruct((batch + 8, batch), F32)],
    )


def join_kernel(_, x_ref, y_ref, *refs):
    refs[-1][...] = x_ref[...] + y_ref[...]


def join(held, x, y, *after):
    return call(
        join_kernel,
        "join",
        (in_vmem(held), x, y, *after),
        vmem(3) + [pl.BlockSpec(memory_space=pl.ANY)] * len(after),
        vmem(1)[0],
        jax.ShapeDtypeStruct(x.shape, x.dtype),
    )


def doublings(axis):
    return [1 << i for i in range(lax.axis_size(axis).bit_length() - 1)]


def swap(x, axis, step):
    return lax.ppermute(x, axis, [(i, i ^ step) for i in range(lax.axis_size(axis))])


def inverse_kernel(_, gram_ref, rewards_ref, inverse_ref, coeffs_ref):
    n = rewards_ref.shape[1]
    lane = lax.broadcasted_iota(jnp.int32, (8, n), 1)
    sub = lax.broadcasted_iota(jnp.int32, (8, n), 0)

    def row(x, t):
        return jnp.broadcast_to(x[t : t + 1, :], (8, n))

    def column(x, t):
        return jnp.broadcast_to(x[:, t : t + 1], (8, n))

    groups = [
        gram_ref[first : first + 8, :] + jnp.where(lane == sub + first, 1.0, 0.0) for first in range(0, n, 8)
    ]
    for g in range(n // 8):
        first = 8 * g
        inside = (lane >= first) & (lane < first + 8)
        eye = jnp.where(lane == sub + first, 1.0, 0.0)
        columns = [column(groups[g], first + t) for t in range(8)]
        swept = jnp.where(inside, eye, groups[g])
        for t in range(8):
            scale = 1.0 / row(columns[t], t)
            factor = columns[t]

            def eliminate(x):
                mine = row(x, t) * scale
                return jnp.where(sub == t, mine, x - factor * mine)

            swept = eliminate(swept)
            for u in range(t + 1, 8):
                columns[u] = eliminate(columns[u])
        swept = jnp.where(inside, -swept, swept)
        rows = [row(swept, t) for t in range(8)]
        order = [h % (n // 8) for h in range(g + 1, g + n // 8)]
        for h in order:
            x = jnp.where(inside, 0.0, groups[h])
            for t in range(8):
                x = x - column(groups[h], first + t) * rows[t]
            groups[h] = x
        groups[g] = swept
    for g in range(n // 8):
        inverse_ref[8 * g : 8 * g + 8, :] = -groups[g]
    gap = jnp.broadcast_to(rewards_ref[...] - gram_ref[n : n + 1, :], (8, n))
    coeffs_ref[...] = lax.dot_general(
        gap,
        inverse_ref[...],
        (((1,), (0,)), ((), ())),
        precision=lax.Precision.HIGHEST,
        preferred_element_type=F32,
    )


def inverse_and_coeffs(held, gram, rewards):
    n = rewards.shape[0]
    return call(
        inverse_kernel,
        "inverse",
        (in_vmem(held), gram, rewards.reshape(1, n)),
        vmem(3),
        vmem(2),
        [jax.ShapeDtypeStruct((n, n), F32), jax.ShapeDtypeStruct((8, n), F32)],
    )


def update_kernel(near, far, *refs):
    c_ref, inverse_ref, coeffs_ref, mean_ref = refs[:4]
    near_refs = refs[4 : 4 + near]
    far_refs = refs[4 + near : 4 + near + far]
    out_ref, new_mean_ref, gain, panel, other, buffers, sems = refs[4 + near + far :]
    outer, inner_index, col, _, cols = places()
    batch = inverse_ref.shape[0]
    quarter = near_refs[0].shape[0]
    for s, part in enumerate(near_refs):
        panel[span(col ^ s, quarter), :] = part[...]
    for s, part in enumerate(far_refs):
        here = span((inner_index ^ (s // cols)) * cols + (outer ^ (s % cols)), quarter)
        other[here, :batch] = part[...]
        other[here, batch:] = part[...]
    hi, lo = split2(inverse_ref[...])
    rows = panel[...]
    product = dot(rows, hi) + dot(rows, lo)
    hi, lo = split2(product)
    gain[:, :batch] = hi
    gain[:, batch:] = lo
    new_mean_ref[...] = mean_ref[...] + sum(dot(p, rows, NT) for p in split3(coeffs_ref[...]))[:1]

    slots, rows, width = buffers.shape
    across = c_ref.shape[1] // width
    steps = c_ref.shape[0] // rows * across

    def copy(n):
        i, j = n // across, n % across
        there = out_ref.at[pl.ds(i * rows, rows), pl.ds(j * width, width)]
        return pltpu.make_async_copy(buffers.at[n % slots], there, sems.at[n % slots])

    for n in range(steps):
        here = pl.ds(n // across * rows, rows)
        there = pl.ds(n % across * width, width)
        if n >= slots:
            copy(n - slots).wait()
        buffers[n % slots] = c_ref[here, there] - dot(gain[here, :], other[there, :], NT)
        copy(n).start()
    for n in range(max(0, steps - slots), steps):
        copy(n).wait()


def update(covariance, inverse, coeffs, mean, near, far):
    rows, cols = covariance.shape
    batch = inverse.shape[0]
    return call(
        functools.partial(update_kernel, len(near), len(far)),
        "update",
        (in_vmem(covariance), inverse, coeffs, mean.reshape(1, rows), *near, *far),
        vmem(4 + len(near) + len(far)),
        [pl.BlockSpec(memory_space=pl.ANY), vmem(1)[0]],
        [jax.ShapeDtypeStruct((rows, cols), F32), jax.ShapeDtypeStruct((1, rows), F32)],
        [
            pltpu.VMEM((rows, 2 * batch), BF16),
            pltpu.VMEM((rows, batch), BF16),
            pltpu.VMEM((cols, 2 * batch), BF16),
            pltpu.VMEM((6, min(512, rows), min(512, cols)), F32),
            pltpu.SemaphoreType.DMA((6,)),
        ],
    )


def per_device(context, weight, feature_bias, covariance, prior_mean, rewards):
    cols = lax.axis_size("col")
    inner = lax.axis_size("row") // cols
    rows, block = covariance.shape
    part = block // inner
    if (part // cols) % 128 or (rows // cols) % 128:
        return plain(context, weight, feature_bias, covariance, prior_mean, rewards)

    blocks = [context] + [swap_col(context, s) for s in range(1, cols)]
    bias = feature_bias.reshape(1, block)
    w_held, blocks[0], bias = hold(weight, context, bias)
    sums = []
    for k in range(inner - 1, -1, -1):
        piece = preact_part(k, blocks, w_held, part)
        sums.append(swap_inner(piece, k) if k else piece)
    pieces = scatter(sums, cols)
    summed = [pieces[0]] + [swap_outer(pieces[s], s) for s in range(cols - 1, 0, -1)]
    token = touch(covariance, pieces[0])
    features = features_of(token, bias, summed)

    shards = [features] + [swap_outer(features, s) for s in range(1, cols)]
    held = covariance
    panel, sent = panel_part(held, shards[:1], [(0, 0)], "first")
    far_features = transpose(sent)
    panel = panel_part(held, shards[1:], [(s, 0) for s in range(1, cols)], "next", panel)
    for k in range(1, inner):
        others = [swap_inner(s, k) for s in shards]
        kind = "last" if k == inner - 1 else "next"
        panel = panel_part(held, others, [(s, k) for s in range(cols)], kind, panel)

    parts = [panel[0]] + [swap_col(panel[s], s) for s in range(1, cols)]
    own_panel, gram = gram_part(held, far_features, prior_mean, parts)
    steps = [("row", step) for step in doublings("row")] + [("col", step) for step in doublings("col")]
    far = [transpose(own_panel, s) for s in range(cols)]
    near = [own_panel] + [swap_col(own_panel, s) for s in range(1, cols)]
    for i, (axis, step) in enumerate(steps):
        gram = join(held, gram, swap(gram, axis, step), *(far + near[1:] if i == len(steps) - 1 else []))
    for k in range(1, inner):
        far += [swap_inner(f, k) for f in far[:cols]]

    inverse, coeffs = inverse_and_coeffs(held, gram, rewards)
    new_cov, new_mean = update(held, inverse, coeffs, prior_mean, near, far)
    return new_cov, new_mean.reshape(rows)


def solution(mesh):
    return jax.shard_map(
        per_device,
        mesh=mesh,
        in_specs=(P("col", "row"), P("row", "col"), P("col"), P("row", "col"), P("row"), P()),
        out_specs=(P("row", "col"), P("row")),
        check_vma=False,
    )
```

```python
import functools

import jax
import jax.numpy as jnp
from jax import lax
from jax.experimental import pallas as pl
from jax.experimental.pallas import tpu as pltpu
from jax.sharding import PartitionSpec as P

F32 = jnp.float32
BF16 = jnp.bfloat16
MIB = 1 << 20
NT = (((1,), (1,)), ((), ()))
TN = (((0,), (0,)), ((), ()))


def dot(a, b, dims=(((1,), (0,)), ((), ()))):
    return lax.dot_general(a, b, dims, preferred_element_type=F32)


def split2(x):
    hi = x.astype(BF16)
    return hi, (x - hi.astype(F32)).astype(BF16)


def split3(x):
    hi = x.astype(BF16)
    rest = x - hi.astype(F32)
    mid = rest.astype(BF16)
    return hi, mid, (rest - mid.astype(F32)).astype(BF16)


def vmem(n):
    return [pl.BlockSpec(memory_space=pltpu.VMEM)] * n


def broadcast(array, axis, root):
    mine = lax.axis_index(axis) == root
    return lax.psum(jnp.where(mine, array, jnp.zeros_like(array)), axis)


def plain(context, weight, feature_bias, covariance, prior_mean, rewards):
    highest = lax.Precision.HIGHEST
    group_ratio = lax.axis_size("row") // lax.axis_size("col")
    row_index = lax.axis_index("row")
    col_index = lax.axis_index("col")
    row_width = covariance.shape[0]
    tokens = lax.all_gather(context, "col", axis=0, tiled=True)
    partial_value = jnp.dot(tokens, weight, preferred_element_type=jnp.float32)
    summed = lax.psum_scatter(partial_value, "row", scatter_dimension=0, tiled=True)
    features = jnp.tanh(summed + feature_bias[None, :]).astype(jnp.bfloat16)
    phi_col = lax.all_gather(features, "row", axis=0, tiled=True)
    phi_held = broadcast(phi_col, "col", row_index // group_ratio)
    phi_row = lax.dynamic_slice_in_dim(phi_held, row_index % group_ratio * row_width, row_width, 1)
    col32 = phi_col.astype(jnp.float32)
    row32 = phi_row.astype(jnp.float32)
    panel_part = jnp.einsum("ik,bk->ib", covariance, col32, precision=highest)
    mean_part = jnp.dot(row32, prior_mean, precision=highest)
    panel = lax.psum(panel_part, "col")
    gram_part = jnp.dot(row32, panel, precision=highest)
    gram_matrix, predicted = lax.psum((gram_part, mean_part), "row")
    order = gram_matrix.shape[0]
    gram_matrix = gram_matrix + jnp.eye(order, dtype=jnp.float32)
    lower_factor = jnp.linalg.cholesky(gram_matrix)
    lower_inverse = lax.linalg.triangular_solve(
        lower_factor, jnp.eye(order, dtype=jnp.float32), left_side=True, lower=True
    )
    inverse_gram = jnp.dot(lower_inverse.T, lower_inverse, precision=highest)
    coeffs = jnp.dot(inverse_gram, rewards - predicted, precision=highest)
    gain_rows = jnp.dot(panel, inverse_gram, precision=highest)
    posterior_mean = prior_mean + jnp.dot(panel, coeffs, precision=highest)
    pieces = []
    for member in range(group_ratio):
        pieces.append(broadcast(panel, "row", col_index * group_ratio + member))
    far_panel = jnp.concatenate(pieces, 0)
    update = jnp.einsum("ib,jb->ij", gain_rows, far_panel, precision=highest)
    posterior_cov = covariance - update
    return (posterior_cov, posterior_mean)


def swap_col(x, step):
    n = lax.axis_size("col")
    return lax.ppermute(x, "col", [(i, i ^ step) for i in range(n)])


def swap_outer(x, step):
    n, inner = lax.axis_size("row"), lax.axis_size("row") // lax.axis_size("col")
    return lax.ppermute(x, "row", [(i, i ^ (step * inner)) for i in range(n)])


def swap_inner(x, step):
    return lax.ppermute(x, "row", [(i, i ^ step) for i in range(lax.axis_size("row"))])


def transpose(x, step=0):
    cols = lax.axis_size("col")
    inner = lax.axis_size("row") // cols
    pairs = []
    for outer in range(cols):
        for k in range(inner):
            for col in range(cols):
                pairs.append(((outer * inner + k) * cols + col, ((col ^ step) * inner + k) * cols + outer))
    return lax.ppermute(x, ("row", "col"), pairs)


def places():
    cols = lax.axis_size("col")
    inner = lax.axis_size("row") // cols
    row = lax.axis_index("row")
    return row // inner, row % inner, lax.axis_index("col"), inner, cols


def span(index, size):
    return pl.ds(pl.multiple_of(index * size, size), size)


def call(kernel, name, operands, in_specs, out_specs, out_shape, scratch_shapes=(), flops=0, size=0):
    return pl.pallas_call(
        kernel,
        in_specs=in_specs,
        out_specs=out_specs,
        out_shape=out_shape,
        scratch_shapes=scratch_shapes,
        cost_estimate=pl.CostEstimate(flops=flops, bytes_accessed=size, transcendentals=0),
        compiler_params=pltpu.CompilerParams(vmem_limit_bytes=14 * MIB),
        name=name,
    )(*operands)


def hold_kernel(*refs):
    n = len(refs) // 2
    copies = [pltpu.make_async_copy(refs[i], refs[n + i], refs[-1].at[i]) for i in range(n)]
    for copy in copies:
        copy.start()
    for copy in copies:
        copy.wait()


def hold(*arrays):
    return call(
        hold_kernel,
        "hold_weight",
        [in_hbm(x) for x in arrays],
        [pl.BlockSpec(memory_space=pl.ANY)] * len(arrays),
        vmem(len(arrays)),
        [pltpu.VMEM(x.shape, x.dtype) for x in arrays[:1]]
        + [jax.ShapeDtypeStruct(x.shape, x.dtype) for x in arrays[1:]],
        [pltpu.SemaphoreType.DMA((len(arrays),))],
        size=arrays[0].size * arrays[0].dtype.itemsize,
    )


def touch_kernel(*refs):
    refs[-1][...] = jnp.zeros_like(refs[-1])


def touch(x, *after):
    return call(
        touch_kernel,
        "touch",
        (in_vmem(x), *after),
        vmem(1) + [pl.BlockSpec(memory_space=pl.ANY)] * len(after),
        vmem(1)[0],
        jax.ShapeDtypeStruct((8, 128), F32),
    )


def in_hbm(x):
    return pltpu.with_memory_space_constraint(x, pltpu.HBM)


def in_vmem(x):
    return pltpu.with_memory_space_constraint(x, pltpu.VMEM)


def preact_kernel(step, *refs):
    *blocks, w_ref, out_ref, held = refs
    _, inner_index, col, _, _ = places()
    rows = blocks[0].shape[0]
    width = out_ref.shape[1]
    tile = min(512, width)
    for s, block in enumerate(blocks):
        held[span(col ^ s, rows), :] = block[...].astype(F32)
    tokens = held[...].astype(BF16)
    first = (inner_index ^ step) * (width // tile)
    for t in range(width // tile):
        out_ref[:, t * tile : (t + 1) * tile] = dot(tokens, w_ref[:, span(first + t, tile)])


def preact_part(step, blocks, weight, width):
    rows, depth = blocks[0].shape
    n = len(blocks)
    return call(
        functools.partial(preact_kernel, step),
        "preact_part",
        (*blocks, in_vmem(weight)),
        vmem(n + 1),
        vmem(1)[0],
        jax.ShapeDtypeStruct((rows * n, width), F32),
        [pltpu.VMEM((rows * n, depth), F32)],
        2 * rows * n * depth * width,
        2 * depth * width,
    )


def scatter_kernel(n, *refs):
    sums, outs = refs[:n], refs[n:]
    outer, *_ = places()
    width = outs[0].shape[1]
    for s, out in enumerate(outs):
        here = span(outer ^ s, width)
        out[...] = sum(x[:, here] for x in sums)


def scatter(sums, count):
    rows, width = sums[0].shape
    shape = jax.ShapeDtypeStruct((rows, width // count), F32)
    return call(
        functools.partial(scatter_kernel, len(sums)), "scatter", sums, vmem(len(sums)), vmem(count), [shape] * count, size=8 * rows * width
    )


def feature_kernel(_, bias_ref, *refs):
    *parts, out_ref = refs
    outer, inner_index, _, _, cols = places()
    here = span(inner_index * cols + outer, out_ref.shape[1])
    out_ref[...] = jnp.tanh(sum(p[...] for p in parts) + bias_ref[:, here]).astype(BF16)


def features_of(token, bias, parts):
    rows, width = parts[0].shape
    return call(
        feature_kernel,
        "features",
        (token, bias, *parts),
        vmem(2 + len(parts)),
        vmem(1)[0],
        jax.ShapeDtypeStruct((rows, width), BF16),
        size=16 * rows * width,
    )


def panel_kernel(steps, kind, c_ref, *refs):
    n = len(steps)
    last = kind == "last"
    shards, rest = refs[:n], refs[n:]
    outer, inner_index, col, _, cols = places()
    acc_ref = None if kind == "first" else rest[0]
    outs = rest[0 if acc_ref is None else 1 :]
    if kind == "first":
        outs[1][...] = shards[0][...]
    width = shards[0].shape[1]
    quarter = c_ref.shape[0] // cols
    rows = min(512, quarter)
    per = quarter // rows
    for q in range(cols):
        block = (col ^ q) if last else q

        @pl.loop(0, per)
        def _(i, q=q, block=block):
            here = span(block * per + i, rows)
            sums = None if acc_ref is None else acc_ref[here, :]
            for shard, (s, k) in zip(shards, steps):
                hi, lo = split2(c_ref[here, span((inner_index ^ k) * cols + (outer ^ s), width)])
                phi = shard[...]
                term = dot(hi, phi, NT) + dot(lo, phi, NT)
                sums = term if sums is None else sums + term
            if last:
                outs[q][span(i, rows), :] = sums.astype(outs[q].dtype)
            else:
                outs[0][here, :] = sums


def panel_part(covariance, shards, steps, kind, acc=None):
    n = len(shards)
    batch, width = shards[0].shape
    rows = covariance.shape[0]
    cols = lax.axis_size("col")
    operands = [in_vmem(covariance), *shards] + ([] if acc is None else [acc])
    shape = [jax.ShapeDtypeStruct((rows, batch), F32)]
    if kind == "last":
        shape = [jax.ShapeDtypeStruct((rows // cols, batch), F32)] * cols
    if kind == "first":
        shape.append(jax.ShapeDtypeStruct((batch, width), BF16))
    outs = call(
        functools.partial(panel_kernel, tuple(steps), kind),
        "panel_part",
        operands,
        vmem(len(operands)),
        vmem(len(shape)),
        shape,
        (),
        4 * rows * width * n * batch,
        4 * rows * width * n,
    )
    return outs if len(shape) > 1 else outs[0]


def gram_kernel(_, phi_ref, mean_ref, *refs):
    *parts, panel_ref, gram_ref = refs
    _, _, col, _, _ = places()
    panel = parts[0][...]
    for part in parts[1:]:
        panel = panel + part[...].astype(F32)
    panel_ref[...] = panel.astype(BF16)
    phi = phi_ref[...]
    batch = phi.shape[0]
    gram_ref[:batch, :] = sum(dot(phi, piece) for piece in split3(panel))
    mean = jnp.broadcast_to(mean_ref[:, span(col, panel.shape[0])], (8, panel.shape[0]))
    gram_ref[batch:, :] = sum(dot(piece, phi, NT) for piece in split3(mean))


def gram_part(held, phi, mean, parts):
    rows, batch = parts[0].shape
    return call(
        gram_kernel,
        "gram_part",
        (in_vmem(held), phi, mean.reshape(1, mean.shape[0]), *parts),
        vmem(3 + len(parts)),
        vmem(2),
        [jax.ShapeDtypeStruct((rows, batch), BF16), jax.ShapeDtypeStruct((batch + 8, batch), F32)],
    )


def join_kernel(_, x_ref, y_ref, *refs):
    refs[-1][...] = x_ref[...] + y_ref[...]


def join(held, x, y, *after):
    return call(
        join_kernel,
        "join",
        (in_vmem(held), x, y, *after),
        vmem(3) + [pl.BlockSpec(memory_space=pl.ANY)] * len(after),
        vmem(1)[0],
        jax.ShapeDtypeStruct(x.shape, x.dtype),
    )


def doublings(axis):
    return [1 << i for i in range(lax.axis_size(axis).bit_length() - 1)]


def swap(x, axis, step):
    return lax.ppermute(x, axis, [(i, i ^ step) for i in range(lax.axis_size(axis))])


def inverse_kernel(_, gram_ref, rewards_ref, inverse_ref, coeffs_ref):
    n = rewards_ref.shape[1]
    lane = lax.broadcasted_iota(jnp.int32, (8, n), 1)
    sub = lax.broadcasted_iota(jnp.int32, (8, n), 0)

    def row(x, t):
        return jnp.broadcast_to(x[t : t + 1, :], (8, n))

    def column(x, t):
        return jnp.broadcast_to(x[:, t : t + 1], (8, n))

    groups = [
        gram_ref[first : first + 8, :] + jnp.where(lane == sub + first, 1.0, 0.0) for first in range(0, n, 8)
    ]
    for g in range(n // 8):
        first = 8 * g
        inside = (lane >= first) & (lane < first + 8)
        eye = jnp.where(lane == sub + first, 1.0, 0.0)
        columns = [column(groups[g], first + t) for t in range(8)]
        swept = jnp.where(inside, eye, groups[g])
        for t in range(8):
            scale = 1.0 / row(columns[t], t)
            factor = columns[t]

            def eliminate(x):
                mine = row(x, t) * scale
                return jnp.where(sub == t, mine, x - factor * mine)

            swept = eliminate(swept)
            for u in range(t + 1, 8):
                columns[u] = eliminate(columns[u])
        swept = jnp.where(inside, -swept, swept)
        rows = [row(swept, t) for t in range(8)]
        order = [h % (n // 8) for h in range(g + 1, g + n // 8)]
        for h in order:
            x = jnp.where(inside, 0.0, groups[h])
            for t in range(8):
                x = x - column(groups[h], first + t) * rows[t]
            groups[h] = x
        groups[g] = swept
    for g in range(n // 8):
        inverse_ref[8 * g : 8 * g + 8, :] = -groups[g]
    gap = jnp.broadcast_to(rewards_ref[...] - gram_ref[n : n + 1, :], (8, n))
    coeffs_ref[...] = lax.dot_general(
        gap,
        inverse_ref[...],
        (((1,), (0,)), ((), ())),
        precision=lax.Precision.HIGHEST,
        preferred_element_type=F32,
    )


def inverse_and_coeffs(held, gram, rewards):
    n = rewards.shape[0]
    return call(
        inverse_kernel,
        "inverse",
        (in_vmem(held), gram, rewards.reshape(1, n)),
        vmem(3),
        vmem(2),
        [jax.ShapeDtypeStruct((n, n), F32), jax.ShapeDtypeStruct((8, n), F32)],
    )


def update_kernel(near, far, *refs):
    c_ref, inverse_ref, coeffs_ref, mean_ref = refs[:4]
    near_refs = refs[4 : 4 + near]
    far_refs = refs[4 + near : 4 + near + far]
    out_ref, new_mean_ref, gain, panel, other, buffers, sems = refs[4 + near + far :]
    outer, inner_index, col, _, cols = places()
    batch = inverse_ref.shape[0]
    quarter = near_refs[0].shape[0]
    for s, part in enumerate(near_refs):
        panel[span(col ^ s, quarter), :] = part[...]
    for s, part in enumerate(far_refs):
        here = span((inner_index ^ (s // cols)) * cols + (outer ^ (s % cols)), quarter)
        other[here, :batch] = part[...]
        other[here, batch:] = part[...]
    inverse = split2(inverse_ref[...])

    slots, rows, width = buffers.shape
    across = c_ref.shape[1] // width
    steps = c_ref.shape[0] // rows * across

    def copy(n):
        i, j = n // across, n % across
        there = out_ref.at[pl.ds(i * rows, rows), pl.ds(j * width, width)]
        return pltpu.make_async_copy(buffers.at[n % slots], there, sems.at[n % slots])

    for n in range(steps):
        here = pl.ds(n // across * rows, rows)
        there = pl.ds(n % across * width, width)
        if n % across == 0:
            mine = panel[here, :]
            hi, lo = split2(sum(dot(mine, piece) for piece in inverse))
            gain[here, :batch] = hi
            gain[here, batch:] = lo
        if n >= slots:
            copy(n - slots).wait()
        buffers[n % slots] = c_ref[here, there] - dot(gain[here, :], other[there, :], NT)
        copy(n).start()
    change = sum(dot(piece, panel[...], NT) for piece in split3(coeffs_ref[...]))
    new_mean_ref[...] = mean_ref[...] + change[:1]
    for n in range(max(0, steps - slots), steps):
        copy(n).wait()


def update(covariance, inverse, coeffs, mean, near, far):
    rows, cols = covariance.shape
    batch = inverse.shape[0]
    return call(
        functools.partial(update_kernel, len(near), len(far)),
        "update",
        (in_vmem(covariance), inverse, coeffs, mean.reshape(1, rows), *near, *far),
        vmem(4 + len(near) + len(far)),
        [pl.BlockSpec(memory_space=pl.ANY), vmem(1)[0]],
        [jax.ShapeDtypeStruct((rows, cols), F32), jax.ShapeDtypeStruct((1, rows), F32)],
        [
            pltpu.VMEM((rows, 2 * batch), BF16),
            pltpu.VMEM((rows, batch), BF16),
            pltpu.VMEM((cols, 2 * batch), BF16),
            pltpu.VMEM((6, min(512, rows), min(512, cols)), F32),
            pltpu.SemaphoreType.DMA((6,)),
        ],
    )


def per_device(context, weight, feature_bias, covariance, prior_mean, rewards):
    cols = lax.axis_size("col")
    inner = lax.axis_size("row") // cols
    rows, block = covariance.shape
    part = block // inner
    if (part // cols) % 128 or (rows // cols) % 128:
        return plain(context, weight, feature_bias, covariance, prior_mean, rewards)

    blocks = [context] + [swap_col(context, s) for s in range(1, cols)]
    bias = feature_bias.reshape(1, block)
    w_held, blocks[0], bias = hold(weight, context, bias)
    sums = []
    for k in range(inner - 1, -1, -1):
        piece = preact_part(k, blocks, w_held, part)
        sums.append(swap_inner(piece, k) if k else piece)
    pieces = scatter(sums, cols)
    summed = [pieces[0]] + [swap_outer(pieces[s], s) for s in range(cols - 1, 0, -1)]
    token = touch(covariance, pieces[0])
    features = features_of(token, bias, summed)

    shards = [features] + [swap_outer(features, s) for s in range(1, cols)]
    held = covariance
    panel, sent = panel_part(held, shards[:1], [(0, 0)], "first")
    far_features = transpose(sent)
    panel = panel_part(held, shards[1:], [(s, 0) for s in range(1, cols)], "next", panel)
    for k in range(1, inner):
        others = [swap_inner(s, k) for s in shards]
        kind = "last" if k == inner - 1 else "next"
        panel = panel_part(held, others, [(s, k) for s in range(cols)], kind, panel)

    parts = [panel[0]] + [swap_col(panel[s], s) for s in range(1, cols)]
    own_panel, gram = gram_part(held, far_features, prior_mean, parts)
    steps = [("row", step) for step in doublings("row")] + [("col", step) for step in doublings("col")]
    far = [transpose(own_panel, s) for s in range(cols)]
    near = [own_panel] + [swap_col(own_panel, s) for s in range(1, cols)]
    for i, (axis, step) in enumerate(steps):
        gram = join(held, gram, swap(gram, axis, step), *(far + near[1:] if i == len(steps) - 1 else []))
    for k in range(1, inner):
        far += [swap_inner(f, k) for f in far[:cols]]

    inverse, coeffs = inverse_and_coeffs(held, gram, rewards)
    new_cov, new_mean = update(held, inverse, coeffs, prior_mean, near, far)
    return new_cov, new_mean.reshape(rows)


def solution(mesh):
    return jax.shard_map(
        per_device,
        mesh=mesh,
        in_specs=(P("col", "row"), P("row", "col"), P("col"), P("row", "col"), P("row"), P()),
        out_specs=(P("row", "col"), P("row")),
        check_vma=False,
    )
```
